1024 devices in a mesh: grp: 16 (over x_hi, z), seq: 16 (over y, core), tp: 4 (over x_lo).
Axes of the slice: x: 8 (x_hi: 2, x_lo: 4; x = x_hi * 4 + x_lo), y: 8, z: 8, core: 2. Of those that a mesh axis runs over, the one named last changes fastest.
Arguments:
- queries: bfloat16 [32768, 8192], P(('grp', 'seq', 'tp')), may hold values from -108 to 108
- key_rows: bfloat16 [32768, 1024], P(('grp', 'seq', 'tp')), may hold values from -4 to 4
- value_rows: bfloat16 [32768, 1024], P(('grp', 'seq', 'tp')), may hold values from -6 to 6
- image_lengths: int32 [16, 4], P('grp'), may hold values from 1 to 1024, 2048 in all within a row
- block_table: int32 [256, 16], P(('grp', 'seq')), may hold values from 0 to 15, as said below
Outputs:
- attended: bfloat16 [32768, 8192], P(('grp', 'seq'), 'tp')
The draws below stay inside these ranges and needn't reach their ends.
Inputs may be any that keep to these rules, and one draw needn't show every extreme that they name: `block_table`: for each shard index and each group, exactly one block of each encoder group's shard is destined to that group.
All inputs are finite; a program needn't handle non-finite values.
Results may differ from the reference program's by a relative error of at most 0.004.
Values may be sent and summed in bfloat16 or wider, within the bound.
No kernel may reach another device: no remote copies, remote signals or barrier semaphores. Data moves between devices by JAX's collectives and lax.ppermute only.
A program may use at most 32 MiB of HBM per device.

```python
import math
import jax
import jax.numpy as jnp
import numpy as np
from jax import lax

HEADS = 64
KVH = 8
HD = 128
IMGS = 4
GROUPS = 16
SHARDS = 16
SEQ = 2048
ROWS = 32768
BLOCK = 8


def shared_draw(key):
    base_key = jax.random.fold_in(key, 811)
    key_values = jnp.clip(jax.random.normal(jax.random.fold_in(base_key, 1), (ROWS, KVH * HD), jnp.float32), -4.0, 4.0)
    return key_values


def draw_queries(key, part):
    drawn = jnp.clip(jax.random.normal(jax.random.fold_in(key, 977), (ROWS, HEADS * HD), jnp.float32), -6.0, 6.0)
    return drawn.astype(jnp.bfloat16)


def draw_key_rows(key, part):
    key_values = shared_draw(key)
    return key_values.astype(jnp.bfloat16)


def draw_block_table(key, part):

    def one_shard(shard_index):
        inner_key = jax.random.fold_in(key, 97 + shard_index)
        row_order = jax.random.permutation(jax.random.fold_in(inner_key, 1), GROUPS)
        column_order = jax.random.permutation(jax.random.fold_in(inner_key, 2), GROUPS)
        return (row_order[:, None] + column_order[None, :]) % GROUPS
    latin_rows = jax.vmap(one_shard)(jnp.arange(SHARDS, dtype=jnp.int32))
    return latin_rows.transpose(1, 0, 2).reshape(GROUPS * SHARDS, GROUPS).astype(jnp.int32)


def level_of(rng, shape, pieces, low, top_value):
    level = 1.0
    for dim, parts in pieces:
        steps = jax.random.uniform(jax.random.fold_in(jax.random.fold_in(rng, 6), dim), (parts,), jnp.float32, low / len(pieces), top_value / len(pieces))
        level = level * jnp.repeat(jnp.exp(steps), shape[dim] // parts).reshape((-1,) + (1,) * (len(shape) - 1 - dim))
    return level


def length_profile(number_of, total, reach, lean):
    loads = [(1 << 20) // math.isqrt(standing ** lean) + 1 for standing in range(2, number_of + 1)]
    surplus, holding = total - reach - (number_of - 1), [1] * (number_of - 1)
    while surplus > 0:
        free = [i for i in range(number_of - 1) if holding[i] < reach]
        mass, budget = sum([loads[i] for i in free]), surplus
        for i in free:
            addition = min(reach - holding[i], max(1, budget * loads[i] // mass), surplus)
            holding[i] = holding[i] + addition
            surplus = surplus - addition
    return np.array([reach] + holding)


def ragged_sizes(key, number_of, total, reach, lean):
    if number_of == 2:
        one = jax.random.randint(key, (), max(1, total - reach), min(reach, total - 1) + 1)
        return jnp.stack([one, total - one])
    tallies = jnp.asarray(length_profile(number_of, total, reach, lean), jnp.int32)
    couples = (number_of - 1) // 2
    donor, sink = tallies[1:1 + 2 * couples:2], tallies[2:2 + 2 * couples:2]
    slack = jnp.minimum(donor - 1, reach - sink)
    shifted = jax.random.randint(jax.random.fold_in(key, 1), (couples,), 0, 1 << 20) % (slack + 1)
    tallies = tallies.at[1:1 + 2 * couples:2].set(donor - shifted).at[2:2 + 2 * couples:2].set(sink + shifted)
    return tallies[jax.random.permutation(jax.random.fold_in(key, 2), number_of)]


def centred(stream_key, dims, deviation, limit, shards=(), kind=jnp.bfloat16):
    loudness = level_of(stream_key, dims, shards, -0.22, 0.18) if shards else 1.0
    values = jax.random.normal(stream_key, dims, jnp.float32) * deviation * loudness
    return jnp.minimum(jnp.maximum(values, -limit), limit).astype(kind)


def setup_inputs(seed: int = 0) -> dict:
    keys = jax.random.split(jax.random.key(seed), 6)
    queries = draw_queries(jax.random.fold_in(keys[5], 71), 0)
    key_rows = draw_key_rows(jax.random.fold_in(keys[5], 71), 0)
    value_rows = centred(keys[2], (ROWS, KVH * HD), 1.0, 6.0, ((0, 1024),))
    image_lengths = jax.vmap(lambda own: ragged_sizes(own, IMGS, SEQ, SEQ // 2, 2))(jax.random.split(keys[3], GROUPS)).reshape((GROUPS, IMGS)).astype(jnp.int32)
    block_table = draw_block_table(jax.random.fold_in(keys[5], 71), 0)
    return dict(queries=queries, key_rows=key_rows, value_rows=value_rows, image_lengths=image_lengths, block_table=block_table)


MASKED_SCORE = -1e+30

def place_rows(matrix, chosen, width):
    blocks = matrix.reshape(GROUPS, SHARDS, GROUPS, BLOCK, width)
    source_ids = jnp.arange(GROUPS, dtype=jnp.int32)[None, :, None]
    shard_ids = jnp.arange(SHARDS, dtype=jnp.int32)[None, None, :]
    picked = blocks[source_ids, shard_ids, chosen]
    return picked.transpose(0, 2, 1, 3, 4).reshape(GROUPS, SEQ, width)

def group_attention(packed):
    query_group, key_group, value_group, lengths_row = packed
    position = jnp.arange(SEQ, dtype=jnp.int32)
    bounds = jnp.cumsum(lengths_row)[:-1].astype(jnp.int32)
    image_id = lax.optimization_barrier(jnp.sum((position[:, None] >= bounds[None, :]).astype(jnp.int32), axis=1))
    visible = (position[None, :] <= position[:, None]) & (image_id[None, :] == image_id[:, None])
    query_split = query_group.reshape(SEQ, KVH, HEADS // KVH, HD).transpose(1, 0, 2, 3)
    key_split = key_group.reshape(SEQ, KVH, HD).transpose(1, 0, 2)
    value_split = value_group.reshape(SEQ, KVH, HD).transpose(1, 0, 2)
    score_scale = 1.0 / math.sqrt(HD)

    def head_group(members):
        query_head, key_head, value_head = members
        scores = jnp.einsum('prd,md->rpm', query_head.astype(jnp.float32), key_head.astype(jnp.float32)) * score_scale
        masked = jnp.where(visible[None], scores, MASKED_SCORE)
        row_peak = lax.optimization_barrier(jnp.max(masked, axis=2, keepdims=True))
        weights = jnp.where(visible[None], jnp.exp(masked - row_peak), 0.0)
        summed = lax.optimization_barrier(jnp.sum(weights, axis=2))
        rounded = lax.optimization_barrier(weights.astype(jnp.bfloat16)).astype(jnp.float32)
        product = jnp.einsum('rpm,md->rpd', rounded, value_head.astype(jnp.float32))
        return product / summed[..., None]
    outputs = lax.map(head_group, (query_split, key_split, value_split))
    return outputs.transpose(2, 0, 1, 3).reshape(SEQ, HEADS * HD).astype(jnp.bfloat16)

def reference(queries, key_rows, value_rows, image_lengths, block_table):
    layout = block_table.reshape(GROUPS, SHARDS, GROUPS)
    slot_ids = jnp.arange(GROUPS, dtype=jnp.int32)
    matches = layout[None] == slot_ids[:, None, None, None]
    chosen = lax.optimization_barrier(jnp.sum(jnp.where(matches, slot_ids[None, None, None, :], 0), axis=3)).astype(jnp.int32)
    placed_q = place_rows(queries, chosen, HEADS * HD)
    placed_k = place_rows(key_rows, chosen, KVH * HD)
    placed_v = place_rows(value_rows, chosen, KVH * HD)
    result = lax.map(group_attention, (placed_q, placed_k, placed_v, image_lengths))
    return result.reshape(ROWS, HEADS * HD)
```

```python
import math

import jax
import jax.numpy as jnp
from jax import lax
from jax.experimental import pallas as pl
from jax.experimental.pallas import tpu as pltpu
from jax.sharding import PartitionSpec as P

HD = 128
HIDDEN = -1e30
CHUNK_HEADS = 4


def attend(scalars, q, own, sib, out, keys, values, bias):
    rows = q.shape[0]
    own_rows, sib_rows = own.shape[0], sib.shape[0]
    kv_heads = own.shape[1] // (2 * HD)
    ratio = q.shape[1] // (HD * kv_heads)
    shard = scalars[0]
    position = shard * rows + lax.broadcasted_iota(jnp.int32, (rows, HD), 0)
    start = jnp.zeros((rows, HD), jnp.int32)
    for j in range(3):
        start = jnp.maximum(start, jnp.where(position >= scalars[1 + j], scalars[1 + j], 0))
    lane = lax.broadcasted_iota(jnp.int32, (rows, HD), 1)
    own_blocks = own_rows // rows
    for b in range((own_rows + sib_rows) // rows):
        back = 2 * b if b < own_blocks else 2 * (b - own_blocks) + 1
        for part in range(rows // HD):
            key = (shard - back) * rows + part * HD + lane
            seen = (key >= start) & (key <= position)
            at = b * rows + part * HD
            bias[:, at : at + HD] = jnp.where(seen, 0.0, HIDDEN)
    factor = math.log2(math.e) / math.sqrt(HD)
    total = own_rows + sib_rows
    values[:, HD:] = jnp.ones((total, HD), jnp.bfloat16)
    for kv in range(kv_heads):
        keys[0:own_rows, :] = own[:, kv * HD : (kv + 1) * HD]
        keys[own_rows:, :] = sib[:, kv * HD : (kv + 1) * HD]
        at = (kv_heads + kv) * HD
        values[0:own_rows, :HD] = own[:, at : at + HD]
        values[own_rows:, :HD] = sib[:, at : at + HD]
        for first in range(0, ratio, CHUNK_HEADS):
            heads = range(kv * ratio + first, kv * ratio + first + CHUNK_HEADS)
            stack = jnp.concatenate([q[:, h * HD : (h + 1) * HD] for h in heads], axis=0)
            scores = lax.dot_general(
                stack, keys[...], (((1,), (1,)), ((), ())), preferred_element_type=jnp.float32
            )
            scores = scores.reshape(CHUNK_HEADS, rows, total) + bias[...][None]
            peak = jnp.max(scores, axis=2, keepdims=True)
            weights = jnp.exp2((scores - peak) * factor).astype(jnp.bfloat16)
            both = jnp.dot(
                weights.reshape(CHUNK_HEADS * rows, total),
                values[...],
                preferred_element_type=jnp.float32,
            )
            normal = (both[:, :HD] / both[:, HD:]).astype(jnp.bfloat16)
            for i, h in enumerate(heads):
                out[:, h * HD : (h + 1) * HD] = normal[i * rows : (i + 1) * rows, :]


def attention(scalars, q, own, sib):
    rows, total = q.shape[0], own.shape[0] + sib.shape[0]
    vmem = pl.BlockSpec(memory_space=pltpu.VMEM)
    return pl.pallas_call(
        attend,
        out_shape=jax.ShapeDtypeStruct(q.shape, jnp.bfloat16),
        in_specs=[pl.BlockSpec(memory_space=pltpu.SMEM), vmem, vmem, vmem],
        out_specs=vmem,
        scratch_shapes=[
            pltpu.VMEM((total, HD), jnp.bfloat16),
            pltpu.VMEM((total, 2 * HD), jnp.bfloat16),
            pltpu.VMEM((rows, total), jnp.float32),
        ],
        compiler_params=pltpu.CompilerParams(vmem_limit_bytes=40 << 20),
        cost_estimate=pl.CostEstimate(
            flops=4 * q.shape[1] * rows * total,
            bytes_accessed=2 * (2 * q.size + own.size + sib.size),
            transcendentals=q.shape[1] // HD * rows * total,
        ),
    )(scalars, q, own, sib)


def shards(queries, key_rows, value_rows, image_lengths, block_table):
    tp, groups, seq = lax.axis_size("tp"), lax.axis_size("grp"), lax.axis_size("seq")
    part = queries.shape[0]
    packed = jnp.stack(
        [
            jnp.concatenate(
                [
                    lax.slice_in_dim(a, t * a.shape[1] // tp, (t + 1) * a.shape[1] // tp, axis=1)
                    for a in (queries, key_rows, value_rows)
                ],
                axis=1,
            )
            for t in range(tp)
        ]
    )
    rows = part * tp
    held = lax.all_to_all(packed, "tp", 0, 0, tiled=True).reshape(rows, packed.shape[2])
    block = rows // groups
    destination = jnp.broadcast_to(block_table[0][:, None], (groups, block)).reshape(rows)
    row = lax.broadcasted_iota(jnp.int32, (rows, rows), 0)
    col = lax.broadcasted_iota(jnp.int32, (rows, rows), 1)
    order = (destination[None, :] == row // block) & (row % block == col % block)
    order = order.astype(jnp.bfloat16)
    q_width = queries.shape[1] // tp
    kv_sorted = jnp.dot(order, held[:, q_width:], preferred_element_type=jnp.float32).astype(jnp.bfloat16)
    q_sorted = jnp.dot(order, held[:, :q_width], preferred_element_type=jnp.float32).astype(jnp.bfloat16)
    kv = lax.all_to_all(kv_sorted.reshape(groups, block, -1), "grp", 0, 0, tiled=True).reshape(rows, -1)
    q = lax.all_to_all(q_sorted.reshape(groups, block, -1), "grp", 0, 0, tiled=True).reshape(rows, -1)

    def ahead(x, chips):
        return lax.ppermute(x, "seq", [(i, i + 2 * chips) for i in range(seq - 2 * chips)])

    back4 = ahead(kv, 4)
    back1 = ahead(kv, 1)
    back23 = ahead(jnp.concatenate([kv, back1], axis=0), 2)
    own = jnp.concatenate([kv, back1, back23, back4], axis=0)
    shard = lax.axis_index("seq")
    given = lax.dynamic_slice_in_dim(own, lax.rem(shard, 2) * rows, 4 * rows, 0)
    sib = lax.ppermute(given, "seq", [(i, i ^ 1) for i in range(seq)])
    lengths = image_lengths[0]
    first = lengths[0]
    second = first + lengths[1]
    third = second + lengths[2]
    scalars = jnp.stack([shard.astype(jnp.int32), first, second, third])
    return attention(scalars, q, own, sib)


def solution(mesh):
    in_specs = (
        P(("grp", "seq", "tp"), None),
        P(("grp", "seq", "tp"), None),
        P(("grp", "seq", "tp"), None),
        P("grp", None),
        P(("grp", "seq"), None),
    )
    out_specs = P(("grp", "seq"), "tp")
    return jax.shard_map(shards, mesh=mesh, in_specs=in_specs, out_specs=out_specs, check_vma=False)
```

```python
import math

import jax
import jax.numpy as jnp
from jax import lax
from jax.experimental import pallas as pl
from jax.experimental.pallas import tpu as pltpu
from jax.sharding import PartitionSpec as P

HD = 128
HIDDEN = -1e30
CHUNK_HEADS = 4


def attend(lengths, q, own, sib, out, keys, values, bias):
    rows = q.shape[0]
    own_rows, sib_rows = own.shape[0], sib.shape[0]
    kv_heads = own.shape[1] // (2 * HD)
    ratio = q.shape[1] // (HD * kv_heads)
    shard = lax.axis_index("seq")
    position = shard * rows + lax.broadcasted_iota(jnp.int32, (rows, HD), 0)
    start = jnp.zeros((rows, HD), jnp.int32)
    bound = 0
    for j in range(lengths.shape[1] - 1):
        bound = bound + lengths[0, j]
        start = jnp.where(position >= bound, bound, start)
    lane = lax.broadcasted_iota(jnp.int32, (rows, HD), 1)
    own_blocks = own_rows // rows
    for b in range((own_rows + sib_rows) // rows):
        back = 2 * b if b < own_blocks else 2 * (b - own_blocks) + 1
        for part in range(rows // HD):
            key = (shard - back) * rows + part * HD + lane
            seen = (key >= start) & (key <= position)
            at = b * rows + part * HD
            bias[:, at : at + HD] = jnp.where(seen, 0.0, HIDDEN)
    factor = math.log2(math.e) / math.sqrt(HD)
    total = own_rows + sib_rows
    values[:, HD:] = jnp.ones((total, HD), jnp.bfloat16)
    for kv in range(kv_heads):
        keys[0:own_rows, :] = own[:, kv * HD : (kv + 1) * HD]
        keys[own_rows:, :] = sib[:, kv * HD : (kv + 1) * HD]
        at = (kv_heads + kv) * HD
        values[0:own_rows, :HD] = own[:, at : at + HD]
        values[own_rows:, :HD] = sib[:, at : at + HD]
        for first in range(0, ratio, CHUNK_HEADS):
            heads = range(kv * ratio + first, kv * ratio + first + CHUNK_HEADS)
            stack = jnp.concatenate([q[:, h * HD : (h + 1) * HD] for h in heads], axis=0)
            scores = lax.dot_general(
                stack, keys[...], (((1,), (1,)), ((), ())), preferred_element_type=jnp.float32
            )
            scores = scores.reshape(CHUNK_HEADS, rows, total) + bias[...][None]
            peak = jnp.max(scores, axis=2, keepdims=True)
            weights = jnp.exp2((scores - peak) * factor).astype(jnp.bfloat16)
            both = jnp.dot(
                weights.reshape(CHUNK_HEADS * rows, total),
                values[...],
                preferred_element_type=jnp.float32,
            )
            normal = (both[:, :HD] / both[:, HD:]).astype(jnp.bfloat16)
            for i, h in enumerate(heads):
                out[:, h * HD : (h + 1) * HD] = normal[i * rows : (i + 1) * rows, :]


def attention(lengths, q, own, sib):
    rows, total = q.shape[0], own.shape[0] + sib.shape[0]
    vmem = pl.BlockSpec(memory_space=pltpu.VMEM)
    return pl.pallas_call(
        attend,
        out_shape=jax.ShapeDtypeStruct(q.shape, jnp.bfloat16),
        in_specs=[pl.BlockSpec(memory_space=pltpu.SMEM), vmem, vmem, vmem],
        out_specs=vmem,
        scratch_shapes=[
            pltpu.VMEM((total, HD), jnp.bfloat16),
            pltpu.VMEM((total, 2 * HD), jnp.bfloat16),
            pltpu.VMEM((rows, total), jnp.float32),
        ],
        compiler_params=pltpu.CompilerParams(vmem_limit_bytes=40 << 20),
        cost_estimate=pl.CostEstimate(
            flops=4 * q.shape[1] * rows * total,
            bytes_accessed=2 * (2 * q.size + own.size + sib.size),
            transcendentals=q.shape[1] // HD * rows * total,
        ),
    )(lengths, q, own, sib)


def pack(arrays, parts):
    widths = [a.shape[1] // parts for a in arrays]

    def kernel(*refs):
        out = refs[-1]
        for t in range(parts):
            at = 0
            for a, width in zip(refs, widths):
                out[t, :, at : at + width] = a[:, t * width : (t + 1) * width]
                at += width

    return pl.pallas_call(
        kernel,
        out_shape=jax.ShapeDtypeStruct((parts, arrays[0].shape[0], sum(widths)), arrays[0].dtype),
        in_specs=[pl.BlockSpec(memory_space=pltpu.VMEM)] * len(arrays),
        out_specs=pl.BlockSpec(memory_space=pltpu.VMEM),
    )(*arrays)


def shards(queries, key_rows, value_rows, image_lengths, block_table):
    tp, groups, seq = lax.axis_size("tp"), lax.axis_size("grp"), lax.axis_size("seq")
    me = lax.axis_index("tp")
    part = queries.shape[0]
    rows = part * tp
    block = rows // groups
    blocks = part // block
    packed = pack((key_rows, value_rows), tp)
    held_kv = lax.all_to_all(packed, "tp", 0, 0, tiled=True).reshape(rows, -1)
    q_width = queries.shape[1] // tp
    pieces, arrived = [], []
    for d in range(tp):
        other = me ^ d
        piece = lax.dynamic_slice_in_dim(queries, other * q_width, q_width, axis=1)
        if d:
            piece = lax.ppermute(piece, "tp", [(i, i ^ d) for i in range(tp)])
        pieces.append(piece)
        arrived.append(lax.dynamic_slice_in_dim(block_table[0], other * blocks, blocks))
    held_q = jnp.concatenate(pieces, axis=0)

    def order(destination):
        wide = jnp.broadcast_to(destination[:, None], (groups, block)).reshape(rows)
        row = lax.broadcasted_iota(jnp.int32, (rows, rows), 0)
        col = lax.broadcasted_iota(jnp.int32, (rows, rows), 1)
        return ((wide[None, :] == row // block) & (row % block == col % block)).astype(jnp.bfloat16)

    def sort(matrix, rows_held):
        out = jnp.dot(matrix, rows_held, preferred_element_type=jnp.float32).astype(jnp.bfloat16)
        return out.reshape(groups, block, -1)

    kv_sorted = sort(order(block_table[0]), held_kv)
    q_sorted = sort(order(jnp.concatenate(arrived)), held_q)
    kv = lax.all_to_all(kv_sorted, "grp", 0, 0, tiled=True).reshape(rows, -1)
    kv, q_sorted = lax.optimization_barrier((kv, q_sorted))
    q = lax.all_to_all(q_sorted, "grp", 0, 0, tiled=True).reshape(rows, -1)

    def ahead(x, chips):
        return lax.ppermute(x, "seq", [(i, i + 2 * chips) for i in range(seq - 2 * chips)])

    back1, back2, back4 = ahead(kv, 1), ahead(kv, 2), ahead(kv, 4)
    own = jnp.concatenate([kv, back1, back2, ahead(back1, 2), back4], axis=0)
    shard = lax.axis_index("seq")
    given = lax.dynamic_slice_in_dim(own, lax.rem(shard, 2) * rows, 4 * rows, 0)
    sib = lax.ppermute(given, "seq", [(i, i ^ 1) for i in range(seq)])
    return attention(image_lengths, q, own, sib)


def solution(mesh):
    in_specs = (
        P(("grp", "seq", "tp"), None),
        P(("grp", "seq", "tp"), None),
        P(("grp", "seq", "tp"), None),
        P("grp", None),
        P(("grp", "seq"), None),
    )
    out_specs = P(("grp", "seq"), "tp")
    return jax.shard_map(shards, mesh=mesh, in_specs=in_specs, out_specs=out_specs, check_vma=False)
```

```python
import math

import jax
import jax.numpy as jnp
from jax import lax
from jax.experimental import pallas as pl
from jax.experimental.pallas import tpu as pltpu
from jax.sharding import PartitionSpec as P

HD = 128
HIDDEN = -1e30
CHUNK_HEADS = 4


def attend(lengths, q, own, sib, out, keys, values, bias):
    rows = q.shape[0]
    own_rows, sib_rows = own.shape[0], sib.shape[0]
    kv_heads = own.shape[1] // (2 * HD)
    ratio = q.shape[1] // (HD * kv_heads)
    shard = lax.axis_index("seq")
    position = shard * rows + lax.broadcasted_iota(jnp.int32, (rows, HD), 0)
    start = jnp.zeros((rows, HD), jnp.int32)
    bound = 0
    for j in range(lengths.shape[1] - 1):
        bound = bound + lengths[0, j]
        start = jnp.where(position >= bound, bound, start)
    lane = lax.broadcasted_iota(jnp.int32, (rows, HD), 1)
    own_blocks = own_rows // rows
    for b in range((own_rows + sib_rows) // rows):
        back = 2 * b if b < own_blocks else 2 * (b - own_blocks) + 1
        for part in range(rows // HD):
            key = (shard - back) * rows + part * HD + lane
            seen = (key >= start) & (key <= position)
            at = b * rows + part * HD
            bias[:, at : at + HD] = jnp.where(seen, 0.0, HIDDEN)
    factor = math.log2(math.e) / math.sqrt(HD)
    total = own_rows + sib_rows
    values[:, HD:] = jnp.ones((total, HD), jnp.bfloat16)
    for kv in range(kv_heads):
        keys[0:own_rows, :] = own[:, kv * HD : (kv + 1) * HD]
        keys[own_rows:, :] = sib[:, kv * HD : (kv + 1) * HD]
        at = (kv_heads + kv) * HD
        values[0:own_rows, :HD] = own[:, at : at + HD]
        values[own_rows:, :HD] = sib[:, at : at + HD]
        for first in range(0, ratio, CHUNK_HEADS):
            heads = range(kv * ratio + first, kv * ratio + first + CHUNK_HEADS)
            stack = jnp.concatenate([q[:, h * HD : (h + 1) * HD] for h in heads], axis=0)
            scores = lax.dot_general(
                stack, keys[...], (((1,), (1,)), ((), ())), preferred_element_type=jnp.float32
            )
            scores = scores.reshape(CHUNK_HEADS, rows, total) + bias[...][None]
            peak = jnp.max(scores, axis=2, keepdims=True)
            weights = jnp.exp2((scores - peak) * factor).astype(jnp.bfloat16)
            both = jnp.dot(
                weights.reshape(CHUNK_HEADS * rows, total),
                values[...],
                preferred_element_type=jnp.float32,
            )
            normal = (both[:, :HD] / both[:, HD:]).astype(jnp.bfloat16)
            for i, h in enumerate(heads):
                out[:, h * HD : (h + 1) * HD] = normal[i * rows : (i + 1) * rows, :]


def attention(lengths, q, own, sib):
    rows, total = q.shape[0], own.shape[0] + sib.shape[0]
    vmem = pl.BlockSpec(memory_space=pltpu.VMEM)
    return pl.pallas_call(
        attend,
        out_shape=jax.ShapeDtypeStruct(q.shape, jnp.bfloat16),
        in_specs=[pl.BlockSpec(memory_space=pltpu.SMEM), vmem, vmem, vmem],
        out_specs=vmem,
        scratch_shapes=[
            pltpu.VMEM((total, HD), jnp.bfloat16),
            pltpu.VMEM((total, 2 * HD), jnp.bfloat16),
            pltpu.VMEM((rows, total), jnp.float32),
        ],
        compiler_params=pltpu.CompilerParams(vmem_limit_bytes=40 << 20),
        cost_estimate=pl.CostEstimate(
            flops=4 * q.shape[1] * rows * total,
            bytes_accessed=2 * (2 * q.size + own.size + sib.size),
            transcendentals=q.shape[1] // HD * rows * total,
        ),
    )(lengths, q, own, sib)


def pack(arrays, parts):
    widths = [a.shape[1] // parts for a in arrays]

    def kernel(*refs):
        out = refs[-1]
        for t in range(parts):
            at = 0
            for a, width in zip(refs, widths):
                out[t, :, at : at + width] = a[:, t * width : (t + 1) * width]
                at += width

    return pl.pallas_call(
        kernel,
        out_shape=jax.ShapeDtypeStruct((parts, arrays[0].shape[0], sum(widths)), arrays[0].dtype),
        in_specs=[pl.BlockSpec(memory_space=pltpu.VMEM)] * len(arrays),
        out_specs=pl.BlockSpec(memory_space=pltpu.VMEM),
    )(*arrays)


def shards(queries, key_rows, value_rows, image_lengths, block_table):
    tp, groups, seq = lax.axis_size("tp"), lax.axis_size("grp"), lax.axis_size("seq")
    me = lax.axis_index("tp")
    part = queries.shape[0]
    rows = part * tp
    block = rows // groups
    blocks = part // block
    packed = pack((key_rows, value_rows), tp)
    held_kv = lax.all_to_all(packed, "tp", 0, 0, tiled=True).reshape(rows, -1)
    q_width = queries.shape[1] // tp
    pieces, arrived = [], []
    for d in range(tp):
        other = me ^ d
        piece = lax.dynamic_slice_in_dim(queries, other * q_width, q_width, axis=1)
        if d:
            piece = lax.ppermute(piece, "tp", [(i, i ^ d) for i in range(tp)])
        pieces.append(piece)
        arrived.append(lax.dynamic_slice_in_dim(block_table[0], other * blocks, blocks))
    held_q = jnp.concatenate(pieces, axis=0)

    def order(destination):
        wide = jnp.broadcast_to(destination[:, None], (groups, block)).reshape(rows)
        row = lax.broadcasted_iota(jnp.int32, (rows, rows), 0)
        col = lax.broadcasted_iota(jnp.int32, (rows, rows), 1)
        return ((wide[None, :] == row // block) & (row % block == col % block)).astype(jnp.bfloat16)

    def sort(matrix, rows_held):
        out = jnp.dot(matrix, rows_held, preferred_element_type=jnp.float32).astype(jnp.bfloat16)
        return out.reshape(groups, block, -1)

    kv_sorted = sort(order(block_table[0]), held_kv)
    q_sorted = sort(order(jnp.concatenate(arrived)), held_q)
    kv = lax.all_to_all(kv_sorted, "grp", 0, 0, tiled=True).reshape(rows, -1)
    kv, q_sorted = lax.optimization_barrier((kv, q_sorted))
    q = lax.all_to_all(q_sorted, "grp", 0, 0, tiled=True).reshape(rows, -1)

    def ahead(x, chips):
        return lax.ppermute(x, "seq", [(i, i + 2 * chips) for i in range(seq - 2 * chips)])

    back2, back1 = ahead(kv, 2), ahead(kv, 1)
    own = jnp.concatenate([kv, back1, back2, ahead(back2, 1), ahead(back2, 2)], axis=0)
    shard = lax.axis_index("seq")
    given = lax.dynamic_slice_in_dim(own, lax.rem(shard, 2) * rows, 4 * rows, 0)
    sib = lax.ppermute(given, "seq", [(i, i ^ 1) for i in range(seq)])
    return attention(image_lengths, q, own, sib)


def solution(mesh):
    in_specs = (
        P(("grp", "seq", "tp"), None),
        P(("grp", "seq", "tp"), None),
        P(("grp", "seq", "tp"), None),
        P("grp", None),
        P(("grp", "seq"), None),
    )
    out_specs = P(("grp", "seq"), "tp")
    return jax.shard_map(shards, mesh=mesh, in_specs=in_specs, out_specs=out_specs, check_vma=False)
```

```python
import math

import jax
import jax.numpy as jnp
from jax import lax
from jax.experimental import pallas as pl
from jax.experimental.pallas import tpu as pltpu
from jax.sharding import PartitionSpec as P

HD = 128
HIDDEN = -1e30
CHUNK_HEADS = 4


def attend(lengths, q, own, sib, out, keys, values, bias):
    rows = q.shape[0]
    own_rows, sib_rows = own.shape[0], sib.shape[0]
    kv_heads = own.shape[1] // (2 * HD)
    ratio = q.shape[1] // (HD * kv_heads)
    shard = lax.axis_index("seq")
    position = shard * rows + lax.broadcasted_iota(jnp.int32, (rows, HD), 0)
    start = jnp.zeros((rows, HD), jnp.int32)
    bound = 0
    for j in range(lengths.shape[1] - 1):
        bound = bound + lengths[0, j]
        start = jnp.where(position >= bound, bound, start)
    lane = lax.broadcasted_iota(jnp.int32, (rows, HD), 1)
    own_blocks = own_rows // rows
    for b in range((own_rows + sib_rows) // rows):
        back = 2 * b if b < own_blocks else 2 * (b - own_blocks) + 1
        for part in range(rows // HD):
            key = (shard - back) * rows + part * HD + lane
            seen = (key >= start) & (key <= position)
            at = b * rows + part * HD
            bias[:, at : at + HD] = jnp.where(seen, 0.0, HIDDEN)
    factor = math.log2(math.e) / math.sqrt(HD)
    total = own_rows + sib_rows
    values[:, HD:] = jnp.ones((total, HD), jnp.bfloat16)
    for kv in range(kv_heads):
        keys[0:own_rows, :] = own[:, kv * HD : (kv + 1) * HD]
        keys[own_rows:, :] = sib[:, kv * HD : (kv + 1) * HD]
        at = (kv_heads + kv) * HD
        values[0:own_rows, :HD] = own[:, at : at + HD]
        values[own_rows:, :HD] = sib[:, at : at + HD]
        for first in range(0, ratio, CHUNK_HEADS):
            heads = range(kv * ratio + first, kv * ratio + first + CHUNK_HEADS)
            stack = jnp.concatenate([q[:, h * HD : (h + 1) * HD] for h in heads], axis=0)
            scores = lax.dot_general(
                stack, keys[...], (((1,), (1,)), ((), ())), preferred_element_type=jnp.float32
            )
            scores = scores.reshape(CHUNK_HEADS, rows, total) + bias[...][None]
            peak = jnp.max(scores, axis=2, keepdims=True)
            weights = jnp.exp2((scores - peak) * factor).astype(jnp.bfloat16)
            both = jnp.dot(
                weights.reshape(CHUNK_HEADS * rows, total),
                values[...],
                preferred_element_type=jnp.float32,
            )
            normal = (both[:, :HD] / both[:, HD:]).astype(jnp.bfloat16)
            for i, h in enumerate(heads):
                out[:, h * HD : (h + 1) * HD] = normal[i * rows : (i + 1) * rows, :]


def attention(lengths, q, own, sib):
    rows, total = q.shape[0], own.shape[0] + sib.shape[0]
    vmem = pl.BlockSpec(memory_space=pltpu.VMEM)
    return pl.pallas_call(
        attend,
        out_shape=jax.ShapeDtypeStruct(q.shape, jnp.bfloat16),
        in_specs=[pl.BlockSpec(memory_space=pltpu.SMEM), vmem, vmem, vmem],
        out_specs=vmem,
        scratch_shapes=[
            pltpu.VMEM((total, HD), jnp.bfloat16),
            pltpu.VMEM((total, 2 * HD), jnp.bfloat16),
            pltpu.VMEM((rows, total), jnp.float32),
        ],
        compiler_params=pltpu.CompilerParams(vmem_limit_bytes=40 << 20),
        cost_estimate=pl.CostEstimate(
            flops=4 * q.shape[1] * rows * total,
            bytes_accessed=2 * (2 * q.size + own.size + sib.size),
            transcendentals=q.shape[1] // HD * rows * total,
        ),
    )(lengths, q, own, sib)


def pack(arrays, parts):
    widths = [a.shape[1] // parts for a in arrays]

    def kernel(*refs):
        out = refs[-1]
        for t in range(parts):
            at = 0
            for a, width in zip(refs, widths):
                out[t, :, at : at + width] = a[:, t * width : (t + 1) * width]
                at += width

    return pl.pallas_call(
        kernel,
        out_shape=jax.ShapeDtypeStruct((parts, arrays[0].shape[0], sum(widths)), arrays[0].dtype),
        in_specs=[pl.BlockSpec(memory_space=pltpu.VMEM)] * len(arrays),
        out_specs=pl.BlockSpec(memory_space=pltpu.VMEM),
    )(*arrays)


def shards(queries, key_rows, value_rows, image_lengths, block_table):
    tp, groups, seq = lax.axis_size("tp"), lax.axis_size("grp"), lax.axis_size("seq")
    me = lax.axis_index("tp")
    part = queries.shape[0]
    rows = part * tp
    block = rows // groups
    blocks = part // block
    packed = pack((key_rows, value_rows), tp)
    held_kv = lax.all_to_all(packed, "tp", 0, 0, tiled=True).reshape(rows, -1)
    q_width = queries.shape[1] // tp
    pieces, arrived = [], []
    for d in range(tp):
        other = me ^ d
        piece = lax.dynamic_slice_in_dim(queries, other * q_width, q_width, axis=1)
        if d:
            piece = lax.ppermute(piece, "tp", [(i, i ^ d) for i in range(tp)])
        pieces.append(piece)
        arrived.append(lax.dynamic_slice_in_dim(block_table[0], other * blocks, blocks))

    def order(destination):
        wide = jnp.broadcast_to(destination[:, None], (groups, block)).reshape(rows)
        row = lax.broadcasted_iota(jnp.int32, (rows, rows), 0)
        col = lax.broadcasted_iota(jnp.int32, (rows, rows), 1)
        return ((wide[None, :] == row // block) & (row % block == col % block)).astype(jnp.bfloat16)

    def sort(matrix, rows_held):
        out = jnp.dot(matrix, rows_held, preferred_element_type=jnp.float32).astype(jnp.bfloat16)
        return out.reshape(groups, block, -1)

    kv_sorted = sort(order(block_table[0]), held_kv)
    kv = lax.all_to_all(kv_sorted, "grp", 0, 0, tiled=True).reshape(rows, -1)
    kv, *pieces = lax.optimization_barrier((kv, *pieces))
    held_q = jnp.concatenate(pieces, axis=0)
    q_sorted = sort(order(jnp.concatenate(arrived)), held_q)
    q = lax.all_to_all(q_sorted, "grp", 0, 0, tiled=True).reshape(rows, -1)

    def ahead(x, chips):
        return lax.ppermute(x, "seq", [(i, i + 2 * chips) for i in range(seq - 2 * chips)])

    back2, back1 = ahead(kv, 2), ahead(kv, 1)
    own = jnp.concatenate([kv, back1, back2, ahead(back2, 1), ahead(back2, 2)], axis=0)
    shard = lax.axis_index("seq")
    given = lax.dynamic_slice_in_dim(own, lax.rem(shard, 2) * rows, 4 * rows, 0)
    sib = lax.ppermute(given, "seq", [(i, i ^ 1) for i in range(seq)])
    return attention(image_lengths, q, own, sib)


def solution(mesh):
    in_specs = (
        P(("grp", "seq", "tp"), None),
        P(("grp", "seq", "tp"), None),
        P(("grp", "seq", "tp"), None),
        P("grp", None),
        P(("grp", "seq"), None),
    )
    out_specs = P(("grp", "seq"), "tp")
    return jax.shard_map(shards, mesh=mesh, in_specs=in_specs, out_specs=out_specs, check_vma=False)
```

```python
import math

import jax
import jax.numpy as jnp
from jax import lax
from jax.experimental import pallas as pl
from jax.experimental.pallas import tpu as pltpu
from jax.sharding import PartitionSpec as P

HD = 128
HIDDEN = -1e30
CHUNK_HEADS = 4


def attend(lengths, q, own, sib, out, keys, values, bias):
    rows = q.shape[0]
    own_rows, sib_rows = own.shape[0], sib.shape[0]
    kv_heads = own.shape[1] // (2 * HD)
    ratio = q.shape[1] // (HD * kv_heads)
    shard = lax.axis_index("seq")
    position = shard * rows + lax.broadcasted_iota(jnp.int32, (rows, HD), 0)
    start = jnp.zeros((rows, HD), jnp.int32)
    bound = 0
    for j in range(lengths.shape[1] - 1):
        bound = bound + lengths[0, j]
        start = jnp.where(position >= bound, bound, start)
    lane = lax.broadcasted_iota(jnp.int32, (rows, HD), 1)
    own_blocks = own_rows // rows
    for b in range((own_rows + sib_rows) // rows):
        back = 2 * b if b < own_blocks else 2 * (b - own_blocks) + 1
        for part in range(rows // HD):
            key = (shard - back) * rows + part * HD + lane
            seen = (key >= start) & (key <= position)
            at = b * rows + part * HD
            bias[:, at : at + HD] = jnp.where(seen, 0.0, HIDDEN)
    factor = math.log2(math.e) / math.sqrt(HD)
    total = own_rows + sib_rows
    values[:, HD:] = jnp.ones((total, HD), jnp.bfloat16)
    for kv in range(kv_heads):
        keys[0:own_rows, :] = own[:, kv * HD : (kv + 1) * HD]
        keys[own_rows:, :] = sib[:, kv * HD : (kv + 1) * HD]
        at = (kv_heads + kv) * HD
        values[0:own_rows, :HD] = own[:, at : at + HD]
        values[own_rows:, :HD] = sib[:, at : at + HD]
        for first in range(0, ratio, CHUNK_HEADS):
            heads = range(kv * ratio + first, kv * ratio + first + CHUNK_HEADS)
            stack = jnp.concatenate([q[:, h * HD : (h + 1) * HD] for h in heads], axis=0)
            scores = lax.dot_general(
                stack, keys[...], (((1,), (1,)), ((), ())), preferred_element_type=jnp.float32
            )
            scores = scores.reshape(CHUNK_HEADS, rows, total) + bias[...][None]
            peak = jnp.max(scores, axis=2, keepdims=True)
            weights = jnp.exp2((scores - peak) * factor).astype(jnp.bfloat16)
            both = jnp.dot(
                weights.reshape(CHUNK_HEADS * rows, total),
                values[...],
                preferred_element_type=jnp.float32,
            )
            normal = (both[:, :HD] / both[:, HD:]).astype(jnp.bfloat16)
            for i, h in enumerate(heads):
                out[:, h * HD : (h + 1) * HD] = normal[i * rows : (i + 1) * rows, :]


def attention(lengths, q, own, sib):
    rows, total = q.shape[0], own.shape[0] + sib.shape[0]
    vmem = pl.BlockSpec(memory_space=pltpu.VMEM)
    return pl.pallas_call(
        attend,
        out_shape=jax.ShapeDtypeStruct(q.shape, jnp.bfloat16),
        in_specs=[pl.BlockSpec(memory_space=pltpu.SMEM), vmem, vmem, vmem],
        out_specs=vmem,
        scratch_shapes=[
            pltpu.VMEM((total, HD), jnp.bfloat16),
            pltpu.VMEM((total, 2 * HD), jnp.bfloat16),
            pltpu.VMEM((rows, total), jnp.float32),
        ],
        compiler_params=pltpu.CompilerParams(vmem_limit_bytes=40 << 20),
        cost_estimate=pl.CostEstimate(
            flops=4 * q.shape[1] * rows * total,
            bytes_accessed=2 * (2 * q.size + own.size + sib.size),
            transcendentals=q.shape[1] // HD * rows * total,
        ),
    )(lengths, q, own, sib)


def pack(arrays, parts):
    widths = [a.shape[1] // parts for a in arrays]

    def kernel(*refs):
        out = refs[-1]
        for t in range(parts):
            at = 0
            for a, width in zip(refs, widths):
                out[t, :, at : at + width] = a[:, t * width : (t + 1) * width]
                at += width

    return pl.pallas_call(
        kernel,
        out_shape=jax.ShapeDtypeStruct((parts, arrays[0].shape[0], sum(widths)), arrays[0].dtype),
        in_specs=[pl.BlockSpec(memory_space=pltpu.VMEM)] * len(arrays),
        out_specs=pl.BlockSpec(memory_space=pltpu.VMEM),
    )(*arrays)


def shards(queries, key_rows, value_rows, image_lengths, block_table):
    tp, groups, seq = lax.axis_size("tp"), lax.axis_size("grp"), lax.axis_size("seq")
    me = lax.axis_index("tp")
    part = queries.shape[0]
    rows = part * tp
    block = rows // groups
    blocks = part // block
    packed = pack((key_rows, value_rows), tp)
    held_kv = lax.all_to_all(packed, "tp", 0, 0, tiled=True).reshape(rows, -1)
    q_width = queries.shape[1] // tp
    def columns(device):
        return lax.dynamic_slice_in_dim(queries, device * q_width, q_width, axis=1)

    half = tp // 2
    away = jnp.concatenate([columns(me ^ d) for d in range(half, tp)], axis=0)
    come = lax.ppermute(away, "tp", [(i, i ^ half) for i in range(tp)])
    near = [[columns(me ^ d), come[d * part : (d + 1) * part]] for d in range(half)]
    distances, pieces = [0, half], list(near[0])
    for d in range(1, half):
        distances += [d, d ^ half]
        pieces += [lax.ppermute(x, "tp", [(i, i ^ d) for i in range(tp)]) for x in near[d]]
    arrived = [lax.dynamic_slice_in_dim(block_table[0], (me ^ d) * blocks, blocks) for d in distances]

    def order(destination):
        wide = jnp.broadcast_to(destination[:, None], (groups, block)).reshape(rows)
        row = lax.broadcasted_iota(jnp.int32, (rows, rows), 0)
        col = lax.broadcasted_iota(jnp.int32, (rows, rows), 1)
        return ((wide[None, :] == row // block) & (row % block == col % block)).astype(jnp.bfloat16)

    def sort(matrix, rows_held):
        out = jnp.dot(matrix, rows_held, preferred_element_type=jnp.float32).astype(jnp.bfloat16)
        return out.reshape(groups, block, -1)

    kv_sorted = sort(order(block_table[0]), held_kv)
    kv = lax.all_to_all(kv_sorted, "grp", 0, 0, tiled=True).reshape(rows, -1)
    kv, *pieces = lax.optimization_barrier((kv, *pieces))
    held_q = jnp.concatenate(pieces, axis=0)
    q_sorted = sort(order(jnp.concatenate(arrived)), held_q)
    q = lax.all_to_all(q_sorted, "grp", 0, 0, tiled=True).reshape(rows, -1)

    def ahead(x, chips):
        return lax.ppermute(x, "seq", [(i, i + 2 * chips) for i in range(seq - 2 * chips)])

    back2, back1 = ahead(kv, 2), ahead(kv, 1)
    own = jnp.concatenate([kv, back1, back2, ahead(back2, 1), ahead(back2, 2)], axis=0)
    shard = lax.axis_index("seq")
    given = lax.dynamic_slice_in_dim(own, lax.rem(shard, 2) * rows, 4 * rows, 0)
    sib = lax.ppermute(given, "seq", [(i, i ^ 1) for i in range(seq)])
    return attention(image_lengths, q, own, sib)


def solution(mesh):
    in_specs = (
        P(("grp", "seq", "tp"), None),
        P(("grp", "seq", "tp"), None),
        P(("grp", "seq", "tp"), None),
        P("grp", None),
        P(("grp", "seq"), None),
    )
    out_specs = P(("grp", "seq"), "tp")
    return jax.shard_map(shards, mesh=mesh, in_specs=in_specs, out_specs=out_specs, check_vma=False)
```

```python
import math

import jax
import jax.numpy as jnp
from jax import lax
from jax.experimental import pallas as pl
from jax.experimental.pallas import tpu as pltpu
from jax.sharding import PartitionSpec as P

HD = 128
HIDDEN = -1e30
CHUNK_HEADS = 4


def attend(lengths, q, own, sib, out, keys, values, bias):
    rows = q.shape[0]
    own_rows, sib_rows = own.shape[0], sib.shape[0]
    kv_heads = own.shape[1] // (2 * HD)
    ratio = q.shape[1] // (HD * kv_heads)
    shard = lax.axis_index("seq")
    position = shard * rows + lax.broadcasted_iota(jnp.int32, (rows, HD), 0)
    start = jnp.zeros((rows, HD), jnp.int32)
    bound = 0
    for j in range(lengths.shape[1] - 1):
        bound = bound + lengths[0, j]
        start = jnp.where(position >= bound, bound, start)
    lane = lax.broadcasted_iota(jnp.int32, (rows, HD), 1)
    own_blocks = own_rows // rows
    for b in range((own_rows + sib_rows) // rows):
        back = 2 * b if b < own_blocks else 2 * (b - own_blocks) + 1
        for part in range(rows // HD):
            key = (shard - back) * rows + part * HD + lane
            seen = (key >= start) & (key <= position)
            at = b * rows + part * HD
            bias[:, at : at + HD] = jnp.where(seen, 0.0, HIDDEN)
    factor = math.log2(math.e) / math.sqrt(HD)
    total = own_rows + sib_rows
    values[:, HD:] = jnp.ones((total, HD), jnp.bfloat16)
    for kv in range(kv_heads):
        keys[0:own_rows, :] = own[:, kv * HD : (kv + 1) * HD]
        keys[own_rows:, :] = sib[:, kv * HD : (kv + 1) * HD]
        at = (kv_heads + kv) * HD
        values[0:own_rows, :HD] = own[:, at : at + HD]
        values[own_rows:, :HD] = sib[:, at : at + HD]
        for first in range(0, ratio, CHUNK_HEADS):
            heads = range(kv * ratio + first, kv * ratio + first + CHUNK_HEADS)
            stack = jnp.concatenate([q[:, h * HD : (h + 1) * HD] for h in heads], axis=0)
            scores = lax.dot_general(
                stack, keys[...], (((1,), (1,)), ((), ())), preferred_element_type=jnp.float32
            )
            scores = scores.reshape(CHUNK_HEADS, rows, total) + bias[...][None]
            peak = jnp.max(scores, axis=2, keepdims=True)
            weights = jnp.exp2((scores - peak) * factor).astype(jnp.bfloat16)
            both = jnp.dot(
                weights.reshape(CHUNK_HEADS * rows, total),
                values[...],
                preferred_element_type=jnp.float32,
            )
            normal = (both[:, :HD] / both[:, HD:]).astype(jnp.bfloat16)
            for i, h in enumerate(heads):
                out[:, h * HD : (h + 1) * HD] = normal[i * rows : (i + 1) * rows, :]


def attention(lengths, q, own, sib):
    rows, total = q.shape[0], own.shape[0] + sib.shape[0]
    vmem = pl.BlockSpec(memory_space=pltpu.VMEM)
    return pl.pallas_call(
        attend,
        out_shape=jax.ShapeDtypeStruct(q.shape, jnp.bfloat16),
        in_specs=[pl.BlockSpec(memory_space=pltpu.SMEM), vmem, vmem, vmem],
        out_specs=vmem,
        scratch_shapes=[
            pltpu.VMEM((total, HD), jnp.bfloat16),
            pltpu.VMEM((total, 2 * HD), jnp.bfloat16),
            pltpu.VMEM((rows, total), jnp.float32),
        ],
        compiler_params=pltpu.CompilerParams(vmem_limit_bytes=40 << 20),
        cost_estimate=pl.CostEstimate(
            flops=4 * q.shape[1] * rows * total,
            bytes_accessed=2 * (2 * q.size + own.size + sib.size),
            transcendentals=q.shape[1] // HD * rows * total,
        ),
    )(lengths, q, own, sib)


def pack(arrays, parts):
    widths = [a.shape[1] // parts for a in arrays]

    def kernel(*refs):
        out = refs[-1]
        for t in range(parts):
            at = 0
            for a, width in zip(refs, widths):
                out[t, :, at : at + width] = a[:, t * width : (t + 1) * width]
                at += width

    return pl.pallas_call(
        kernel,
        out_shape=jax.ShapeDtypeStruct((parts, arrays[0].shape[0], sum(widths)), arrays[0].dtype),
        in_specs=[pl.BlockSpec(memory_space=pltpu.VMEM)] * len(arrays),
        out_specs=pl.BlockSpec(memory_space=pltpu.VMEM),
    )(*arrays)


def shards(queries, key_rows, value_rows, image_lengths, block_table):
    tp, groups, seq = lax.axis_size("tp"), lax.axis_size("grp"), lax.axis_size("seq")
    me = lax.axis_index("tp")
    part = queries.shape[0]
    rows = part * tp
    block = rows // groups
    blocks = part // block
    packed = pack((key_rows, value_rows), tp)
    held_kv = lax.all_to_all(packed, "tp", 0, 0, tiled=True).reshape(rows, -1)
    q_width = queries.shape[1] // tp
    pieces, arrived = [], []
    for d in range(tp):
        other = me ^ d
        piece = lax.dynamic_slice_in_dim(queries, other * q_width, q_width, axis=1)
        if d:
            piece = lax.ppermute(piece, "tp", [(i, i ^ d) for i in range(tp)])
        pieces.append(piece)
        arrived.append(lax.dynamic_slice_in_dim(block_table[0], other * blocks, blocks))

    def order(destination):
        wide = jnp.broadcast_to(destination[:, None], (groups, block)).reshape(rows)
        row = lax.broadcasted_iota(jnp.int32, (rows, rows), 0)
        col = lax.broadcasted_iota(jnp.int32, (rows, rows), 1)
        return ((wide[None, :] == row // block) & (row % block == col % block)).astype(jnp.bfloat16)

    def sort(matrix, rows_held):
        out = jnp.dot(matrix, rows_held, preferred_element_type=jnp.float32).astype(jnp.bfloat16)
        return out.reshape(groups, block, -1)

    kv_sorted = sort(order(block_table[0]), held_kv)
    kv = lax.all_to_all(kv_sorted, "grp", 0, 0, tiled=True).reshape(rows, -1)
    def ahead(x, chips):
        return lax.ppermute(x, "seq", [(i, i + 2 * chips) for i in range(seq - 2 * chips)])

    back2, back1 = ahead(kv, 2), ahead(kv, 1)
    back1, *pieces = lax.optimization_barrier((back1, *pieces))
    held_q = jnp.concatenate(pieces, axis=0)
    q_sorted = sort(order(jnp.concatenate(arrived)), held_q)
    q = lax.all_to_all(q_sorted, "grp", 0, 0, tiled=True).reshape(rows, -1)

    own = jnp.concatenate([kv, back1, back2, ahead(back2, 1), ahead(back2, 2)], axis=0)
    shard = lax.axis_index("seq")
    given = lax.dynamic_slice_in_dim(own, lax.rem(shard, 2) * rows, 4 * rows, 0)
    sib = lax.ppermute(given, "seq", [(i, i ^ 1) for i in range(seq)])
    return attention(image_lengths, q, own, sib)


def solution(mesh):
    in_specs = (
        P(("grp", "seq", "tp"), None),
        P(("grp", "seq", "tp"), None),
        P(("grp", "seq", "tp"), None),
        P("grp", None),
        P(("grp", "seq"), None),
    )
    out_specs = P(("grp", "seq"), "tp")
    return jax.shard_map(shards, mesh=mesh, in_specs=in_specs, out_specs=out_specs, check_vma=False)
```

```python
import math

import jax
import jax.numpy as jnp
from jax import lax
from jax.experimental import pallas as pl
from jax.experimental.pallas import tpu as pltpu
from jax.sharding import PartitionSpec as P

HD = 128
BLOCK = 8
HIDDEN = -1e30
CHUNK_HEADS = 4


def attend(lengths, q, own, sib, out, keys, values, bias):
    rows = q.shape[0]
    own_rows, sib_rows = own.shape[0], sib.shape[0]
    kv_heads = own.shape[1] // (2 * HD)
    ratio = q.shape[1] // (HD * kv_heads)
    shard = lax.axis_index("seq")
    position = shard * rows + lax.broadcasted_iota(jnp.int32, (rows, HD), 0)
    start = jnp.zeros((rows, HD), jnp.int32)
    bound = 0
    for j in range(lengths.shape[1] - 1):
        bound = bound + lengths[0, j]
        start = jnp.where(position >= bound, bound, start)
    lane = lax.broadcasted_iota(jnp.int32, (rows, HD), 1)
    own_blocks = own_rows // rows
    for b in range((own_rows + sib_rows) // rows):
        back = 2 * b if b < own_blocks else 2 * (b - own_blocks) + 1
        for part in range(rows // HD):
            key = (shard - back) * rows + part * HD + lane
            seen = (key >= start) & (key <= position)
            at = b * rows + part * HD
            bias[:, at : at + HD] = jnp.where(seen, 0.0, HIDDEN)
    factor = math.log2(math.e) / math.sqrt(HD)
    total = own_rows + sib_rows
    values[:, HD:] = jnp.ones((total, HD), jnp.bfloat16)
    for kv in range(kv_heads):
        keys[0:own_rows, :] = own[:, kv * HD : (kv + 1) * HD]
        keys[own_rows:, :] = sib[:, kv * HD : (kv + 1) * HD]
        at = (kv_heads + kv) * HD
        values[0:own_rows, :HD] = own[:, at : at + HD]
        values[own_rows:, :HD] = sib[:, at : at + HD]
        for first in range(0, ratio, CHUNK_HEADS):
            heads = range(kv * ratio + first, kv * ratio + first + CHUNK_HEADS)
            stack = jnp.concatenate([q[:, h * HD : (h + 1) * HD] for h in heads], axis=0)
            scores = lax.dot_general(
                stack, keys[...], (((1,), (1,)), ((), ())), preferred_element_type=jnp.float32
            )
            scores = scores.reshape(CHUNK_HEADS, rows, total) + bias[...][None]
            peak = jnp.max(scores, axis=2, keepdims=True)
            weights = jnp.exp2((scores - peak) * factor).astype(jnp.bfloat16)
            both = jnp.dot(
                weights.reshape(CHUNK_HEADS * rows, total),
                values[...],
                preferred_element_type=jnp.float32,
            )
            normal = (both[:, :HD] / both[:, HD:]).astype(jnp.bfloat16)
            for i, h in enumerate(heads):
                out[:, h * HD : (h + 1) * HD] = normal[i * rows : (i + 1) * rows, :]


def attention(lengths, q, own, sib):
    rows, total = q.shape[0], own.shape[0] + sib.shape[0]
    vmem = pl.BlockSpec(memory_space=pltpu.VMEM)
    return pl.pallas_call(
        attend,
        out_shape=jax.ShapeDtypeStruct(q.shape, jnp.bfloat16),
        in_specs=[pl.BlockSpec(memory_space=pltpu.SMEM), vmem, vmem, vmem],
        out_specs=vmem,
        scratch_shapes=[
            pltpu.VMEM((total, HD), jnp.bfloat16),
            pltpu.VMEM((total, 2 * HD), jnp.bfloat16),
            pltpu.VMEM((rows, total), jnp.float32),
        ],
        compiler_params=pltpu.CompilerParams(vmem_limit_bytes=40 << 20),
        cost_estimate=pl.CostEstimate(
            flops=4 * q.shape[1] * rows * total,
            bytes_accessed=2 * (2 * q.size + own.size + sib.size),
            transcendentals=q.shape[1] // HD * rows * total,
        ),
    )(lengths, q, own, sib)


def pack(arrays, table, parts):
    widths = [a.shape[1] // parts for a in arrays]
    part = arrays[0].shape[0]
    rows = part * parts

    def kernel(table, *refs):
        *held, out, order, turned = refs
        me = lax.axis_index("tp")
        for t in range(parts):
            at = 0
            for a, width in zip(held, widths):
                out[t, :, at : at + width] = a[:, t * width : (t + 1) * width]
                at += width
        row = lax.broadcasted_iota(jnp.int32, (rows, rows), 0)
        col = lax.broadcasted_iota(jnp.int32, (rows, rows), 1)
        source = col // BLOCK
        for matrix, first in ((order, 0), (turned, me)):
            wanted = jnp.zeros((rows, rows), jnp.int32)
            for b in range(rows // BLOCK):
                d, inner = divmod(b, part // BLOCK)
                wanted = jnp.where(source == b, table[0, (first ^ d) * (part // BLOCK) + inner] * BLOCK, wanted)
            matrix[...] = jnp.where(row == wanted + col % BLOCK, 1.0, 0.0).astype(matrix.dtype)

    dtype = arrays[0].dtype
    vmem = pl.BlockSpec(memory_space=pltpu.VMEM)
    return pl.pallas_call(
        kernel,
        out_shape=[
            jax.ShapeDtypeStruct((parts, part, sum(widths)), dtype),
            jax.ShapeDtypeStruct((rows, rows), dtype),
            jax.ShapeDtypeStruct((rows, rows), dtype),
        ],
        in_specs=[pl.BlockSpec(memory_space=pltpu.SMEM)] + [vmem] * len(arrays),
        out_specs=[vmem] * 3,
    )(table, *arrays)


def shards(queries, key_rows, value_rows, image_lengths, block_table):
    tp, groups, seq = lax.axis_size("tp"), lax.axis_size("grp"), lax.axis_size("seq")
    me = lax.axis_index("tp")
    part = queries.shape[0]
    rows = part * tp
    block = rows // groups
    packed, kv_order, q_order = pack((key_rows, value_rows), block_table, tp)
    held_kv = lax.all_to_all(packed, "tp", 0, 0, tiled=True).reshape(rows, -1)
    q_width = queries.shape[1] // tp
    pieces = []
    for d in range(tp):
        other = me ^ d
        piece = lax.dynamic_slice_in_dim(queries, other * q_width, q_width, axis=1)
        if d:
            piece = lax.ppermute(piece, "tp", [(i, i ^ d) for i in range(tp)])
        pieces.append(piece)
    held_q = jnp.concatenate(pieces, axis=0)

    def sort(matrix, rows_held):
        out = jnp.dot(matrix, rows_held, preferred_element_type=jnp.float32).astype(jnp.bfloat16)
        return out.reshape(groups, block, -1)

    kv_sorted = sort(kv_order, held_kv)
    q_sorted = sort(q_order, held_q)
    kv = lax.all_to_all(kv_sorted, "grp", 0, 0, tiled=True).reshape(rows, -1)
    kv, q_sorted = lax.optimization_barrier((kv, q_sorted))
    q = lax.all_to_all(q_sorted, "grp", 0, 0, tiled=True).reshape(rows, -1)

    def ahead(x, chips):
        return lax.ppermute(x, "seq", [(i, i + 2 * chips) for i in range(seq - 2 * chips)])

    back2, back1 = ahead(kv, 2), ahead(kv, 1)
    own = jnp.concatenate([kv, back1, back2, ahead(back2, 1), ahead(back2, 2)], axis=0)
    shard = lax.axis_index("seq")
    given = lax.dynamic_slice_in_dim(own, lax.rem(shard, 2) * rows, 4 * rows, 0)
    sib = lax.ppermute(given, "seq", [(i, i ^ 1) for i in range(seq)])
    return attention(image_lengths, q, own, sib)


def solution(mesh):
    in_specs = (
        P(("grp", "seq", "tp"), None),
        P(("grp", "seq", "tp"), None),
        P(("grp", "seq", "tp"), None),
        P("grp", None),
        P(("grp", "seq"), None),
    )
    out_specs = P(("grp", "seq"), "tp")
    return jax.shard_map(shards, mesh=mesh, in_specs=in_specs, out_specs=out_specs, check_vma=False)
```

```python
import math

import jax
import jax.numpy as jnp
from jax import lax
from jax.experimental import pallas as pl
from jax.experimental.pallas import tpu as pltpu
from jax.sharding import PartitionSpec as P

HD = 128
BLOCK = 8
HIDDEN = -1e30
CHUNK_HEADS = 4


def attend(lengths, q, own, sib, out, keys, values, bias):
    rows = q.shape[0]
    own_rows, sib_rows = own.shape[0], sib.shape[0]
    kv_heads = own.shape[1] // (2 * HD)
    ratio = q.shape[1] // (HD * kv_heads)
    shard = lax.axis_index("seq")
    position = shard * rows + lax.broadcasted_iota(jnp.int32, (rows, HD), 0)
    start = jnp.zeros((rows, HD), jnp.int32)
    bound = 0
    for j in range(lengths.shape[1] - 1):
        bound = bound + lengths[0, j]
        start = jnp.where(position >= bound, bound, start)
    lane = lax.broadcasted_iota(jnp.int32, (rows, HD), 1)
    own_blocks = own_rows // rows
    for b in range((own_rows + sib_rows) // rows):
        back = 2 * b if b < own_blocks else 2 * (b - own_blocks) + 1
        for part in range(rows // HD):
            key = (shard - back) * rows + part * HD + lane
            seen = (key >= start) & (key <= position)
            at = b * rows + part * HD
            bias[:, at : at + HD] = jnp.where(seen, 0.0, HIDDEN)
    factor = math.log2(math.e) / math.sqrt(HD)
    total = own_rows + sib_rows
    values[:, HD:] = jnp.ones((total, HD), jnp.bfloat16)
    for kv in range(kv_heads):
        keys[0:own_rows, :] = own[:, kv * HD : (kv + 1) * HD]
        keys[own_rows:, :] = sib[:, kv * HD : (kv + 1) * HD]
        at = (kv_heads + kv) * HD
        values[0:own_rows, :HD] = own[:, at : at + HD]
        values[own_rows:, :HD] = sib[:, at : at + HD]
        for first in range(0, ratio, CHUNK_HEADS):
            heads = range(kv * ratio + first, kv * ratio + first + CHUNK_HEADS)
            stack = jnp.concatenate([q[:, h * HD : (h + 1) * HD] for h in heads], axis=0)
            scores = lax.dot_general(
                stack, keys[...], (((1,), (1,)), ((), ())), preferred_element_type=jnp.float32
            )
            scores = scores.reshape(CHUNK_HEADS, rows, total) + bias[...][None]
            peak = jnp.max(scores, axis=2, keepdims=True)
            weights = jnp.exp2((scores - peak) * factor).astype(jnp.bfloat16)
            both = jnp.dot(
                weights.reshape(CHUNK_HEADS * rows, total),
                values[...],
                preferred_element_type=jnp.float32,
            )
            normal = (both[:, :HD] / both[:, HD:]).astype(jnp.bfloat16)
            for i, h in enumerate(heads):
                out[:, h * HD : (h + 1) * HD] = normal[i * rows : (i + 1) * rows, :]


def attention(lengths, q, own, sib):
    rows, total = q.shape[0], own.shape[0] + sib.shape[0]
    vmem = pl.BlockSpec(memory_space=pltpu.VMEM)
    return pl.pallas_call(
        attend,
        out_shape=jax.ShapeDtypeStruct(q.shape, jnp.bfloat16),
        in_specs=[pl.BlockSpec(memory_space=pltpu.SMEM), vmem, vmem, vmem],
        out_specs=vmem,
        scratch_shapes=[
            pltpu.VMEM((total, HD), jnp.bfloat16),
            pltpu.VMEM((total, 2 * HD), jnp.bfloat16),
            pltpu.VMEM((rows, total), jnp.float32),
        ],
        compiler_params=pltpu.CompilerParams(vmem_limit_bytes=40 << 20),
        cost_estimate=pl.CostEstimate(
            flops=4 * q.shape[1] * rows * total,
            bytes_accessed=2 * (2 * q.size + own.size + sib.size),
            transcendentals=q.shape[1] // HD * rows * total,
        ),
    )(lengths, q, own, sib)


def pack(arrays, queries, table, parts):
    widths = [a.shape[1] // parts for a in arrays]
    part = arrays[0].shape[0]
    rows = part * parts

    width_q = queries.shape[1] // parts

    def kernel(table, q, *refs):
        held, (out, order, turned, *pieces) = refs[: len(arrays)], refs[len(arrays) :]
        me = lax.axis_index("tp")
        for d, piece in enumerate(pieces):
            piece[...] = q[:, pl.ds(pl.multiple_of((me ^ d) * width_q, width_q), width_q)]
        for t in range(parts):
            at = 0
            for a, width in zip(held, widths):
                out[t, :, at : at + width] = a[:, t * width : (t + 1) * width]
                at += width
        row = lax.broadcasted_iota(jnp.int32, (rows, rows), 0)
        col = lax.broadcasted_iota(jnp.int32, (rows, rows), 1)
        source = col // BLOCK
        for matrix, first in ((order, 0), (turned, me)):
            wanted = jnp.zeros((rows, rows), jnp.int32)
            for b in range(rows // BLOCK):
                d, inner = divmod(b, part // BLOCK)
                wanted = jnp.where(source == b, table[0, (first ^ d) * (part // BLOCK) + inner] * BLOCK, wanted)
            matrix[...] = jnp.where(row == wanted + col % BLOCK, 1.0, 0.0).astype(matrix.dtype)

    dtype = arrays[0].dtype
    vmem = pl.BlockSpec(memory_space=pltpu.VMEM)
    return pl.pallas_call(
        kernel,
        out_shape=[
            jax.ShapeDtypeStruct((parts, part, sum(widths)), dtype),
            jax.ShapeDtypeStruct((rows, rows), dtype),
            jax.ShapeDtypeStruct((rows, rows), dtype),
        ]
        + [jax.ShapeDtypeStruct((part, width_q), dtype)] * parts,
        in_specs=[pl.BlockSpec(memory_space=pltpu.SMEM)] + [vmem] * (1 + len(arrays)),
        out_specs=[vmem] * (3 + parts),
    )(table, queries, *arrays)


def shards(queries, key_rows, value_rows, image_lengths, block_table):
    tp, groups, seq = lax.axis_size("tp"), lax.axis_size("grp"), lax.axis_size("seq")
    part = queries.shape[0]
    rows = part * tp
    block = rows // groups
    packed, kv_order, q_order, *split = pack((key_rows, value_rows), queries, block_table, tp)
    held_kv = lax.all_to_all(packed, "tp", 0, 0, tiled=True).reshape(rows, -1)
    pieces = []
    for d in range(tp):
        piece = split[d]
        if d:
            piece = lax.ppermute(piece, "tp", [(i, i ^ d) for i in range(tp)])
        pieces.append(piece)
    held_q = jnp.concatenate(pieces, axis=0)

    def sort(matrix, rows_held):
        out = jnp.dot(matrix, rows_held, preferred_element_type=jnp.float32).astype(jnp.bfloat16)
        return out.reshape(groups, block, -1)

    kv_sorted = sort(kv_order, held_kv)
    q_sorted = sort(q_order, held_q)
    kv = lax.all_to_all(kv_sorted, "grp", 0, 0, tiled=True).reshape(rows, -1)
    kv, q_sorted = lax.optimization_barrier((kv, q_sorted))
    q = lax.all_to_all(q_sorted, "grp", 0, 0, tiled=True).reshape(rows, -1)

    def ahead(x, chips):
        return lax.ppermute(x, "seq", [(i, i + 2 * chips) for i in range(seq - 2 * chips)])

    back2, back1 = ahead(kv, 2), ahead(kv, 1)
    own = jnp.concatenate([kv, back1, back2, ahead(back2, 1), ahead(back2, 2)], axis=0)
    shard = lax.axis_index("seq")
    given = lax.dynamic_slice_in_dim(own, lax.rem(shard, 2) * rows, 4 * rows, 0)
    sib = lax.ppermute(given, "seq", [(i, i ^ 1) for i in range(seq)])
    return attention(image_lengths, q, own, sib)


def solution(mesh):
    in_specs = (
        P(("grp", "seq", "tp"), None),
        P(("grp", "seq", "tp"), None),
        P(("grp", "seq", "tp"), None),
        P("grp", None),
        P(("grp", "seq"), None),
    )
    out_specs = P(("grp", "seq"), "tp")
    return jax.shard_map(shards, mesh=mesh, in_specs=in_specs, out_specs=out_specs, check_vma=False)
```
